512 devices in a mesh: train: 16 (over z_lo, y), induce: 32 (over x, z_hi, core).
Axes of the slice: x: 4, y: 4, z: 16 (z_hi: 4, z_lo: 4; z = z_hi * 4 + z_lo), core: 2. Of those that a mesh axis runs over, the one named last changes fastest.
Arguments:
- train_coords: float32 [1024, 192], P('train'), may hold values from -0.3 to 4.8, as said below
- induce_coords: float32 [4096, 192], P('induce'), may hold values from -0.3 to 4.8, as said below
- train_forces: float32 [1024, 192], P('train'), may hold values from -18 to 18
- atom_pairs: int32 [2, 2016], replicated, may hold values from 0 to 63, as said below
- length_scale: float32 [1], replicated, may hold values from 1.5 to 3
Outputs:
- coefficients: float32 [4096, 192], P('induce')
- residual: float32 [4096, 192], P('induce')
- desc_coeffs: float32 [4096, 2016], P('induce')
The draws below stay inside these ranges and needn't reach their ends.
Inputs may be any that keep to these rules, and one draw needn't show every extreme that they name: `atom_pairs`: every unordered pair of two different atoms of the 64 stands in exactly one column, in either order. `train_coords`: atom a lies within 0.3 of 1.5 * (a % 4, a // 4 % 4, a // 16) in each component. `induce_coords`: atom a lies within 0.3 of 1.5 * (a % 4, a // 4 % 4, a // 16) in each component.
All inputs are finite; a program needn't handle non-finite values.
Results may differ from the reference program's by a relative error of at most 0.0085.
Values sent between devices are 32-bit elements; how exact they have to be, the bound alone decides.
A program may use at most 64 MiB of HBM per device.

```python
import math
import jax
import jax.numpy as jnp
import numpy as np
from jax import lax

ATOMS = 64
DESC = 2016
COMP = 192
TRAIN_DEV = 64
STEPS = 2
TRAIN_ALL = 1024
INDUCE_ALL = 4096
N_TRAIN = 16


def geometry_draw(key, row_count):
    atom_ids = jnp.arange(ATOMS, dtype=jnp.int32)
    lattice = 1.5 * jnp.stack([atom_ids % 4, atom_ids // 4 % 4, atom_ids // 16]).astype(jnp.float32)
    jitter = jax.random.uniform(key, (row_count, 3, ATOMS), jnp.float32, -0.3, 0.3)
    return (lattice[None, :, :] + jitter).reshape(row_count, 3 * ATOMS)


def draw_train_coords(key, part):
    return geometry_draw(jax.random.fold_in(key, 11), TRAIN_ALL)


def draw_induce_coords(key, part):
    return geometry_draw(jax.random.fold_in(key, 23), INDUCE_ALL)


def draw_train_forces(key, part):
    row_pos = jnp.arange(TRAIN_ALL, dtype=jnp.float32) / max(TRAIN_ALL - 1, 1)
    inner_key = jax.random.fold_in(key, 43)
    row_scale = 1.0 + 2.0 * row_pos
    noise = jnp.clip(jax.random.normal(inner_key, (TRAIN_ALL, COMP), jnp.float32), -6.0, 6.0)
    return noise * row_scale[:, None]


def draw_atom_pairs(key, part):
    lower_atom, upper_atom = np.triu_indices(ATOMS, 1)
    shuffled = jax.random.permutation(jax.random.fold_in(key, 31), DESC)
    flipped = jax.random.randint(jax.random.fold_in(key, 37), (DESC,), 0, 2)
    head_atom = jnp.asarray(lower_atom, jnp.int32)[shuffled]
    tail_atom = jnp.asarray(upper_atom, jnp.int32)[shuffled]
    first_row = jnp.where(flipped == 1, tail_atom, head_atom)
    second_row = jnp.where(flipped == 1, head_atom, tail_atom)
    return jnp.stack([first_row, second_row]).astype(jnp.int32)


def setup_inputs(seed: int = 0) -> dict:
    key_of = jax.random.split(jax.random.key(seed), 6)
    train_coords = draw_train_coords(jax.random.fold_in(key_of[5], 71), 0)
    induce_coords = draw_induce_coords(jax.random.fold_in(key_of[5], 71), 0)
    train_forces = draw_train_forces(jax.random.fold_in(key_of[5], 71), 0)
    atom_pairs = draw_atom_pairs(jax.random.fold_in(key_of[5], 71), 0)
    length_scale = jnp.clip(jax.random.uniform(key_of[4], (1,), jnp.float32, 1.5, 3.0), 1.5, 3.0)
    return dict(train_coords=train_coords, induce_coords=induce_coords, train_forces=train_forces, atom_pairs=atom_pairs, length_scale=length_scale)


root_five = math.sqrt(5.0)

def make_incidence(atom_pairs, atom_count):
    atom_ids = jnp.arange(atom_count, dtype=jnp.int32)
    head_hit = (atom_pairs[0][:, None] == atom_ids[None, :]).astype(jnp.float32)
    tail_hit = (atom_pairs[1][:, None] == atom_ids[None, :]).astype(jnp.float32)
    return head_hit - tail_hit

def lattice_coords(atom_count):
    atom_ids = jnp.arange(atom_count, dtype=jnp.int32)
    lattice = jnp.stack([atom_ids % 4, atom_ids // 4 % 4, atom_ids // 16]).astype(jnp.float32)
    return (1.5 * lattice).reshape(1, 3 * atom_count)

def describe(coords, incidence):
    atom_count = incidence.shape[1]
    spatial = coords.reshape(coords.shape[0], 3, atom_count)
    offsets = jnp.einsum('bca,pa->bcp', spatial, incidence, precision=lax.Precision.HIGHEST)
    length = jnp.sqrt(lax.optimization_barrier(jnp.sum(offsets * offsets, axis=1)))
    return (1.0 / length, offsets / (length ** 3)[:, None, :])

def centered(coords, incidence):
    values, gradients = describe(coords, incidence)
    lattice_values = describe(lattice_coords(incidence.shape[1]), incidence)[0]
    return ((values - lattice_values).astype(jnp.bfloat16), gradients)

def to_desc(gradients, vectors, incidence):
    atom_count = incidence.shape[1]
    shifted = jnp.einsum('bca,pa->bcp', vectors.reshape(vectors.shape[0], 3, atom_count), incidence, precision=lax.Precision.HIGHEST)
    return -lax.optimization_barrier(jnp.sum(gradients * shifted, axis=1))

def to_forces(gradients, values, incidence):
    weighted = gradients * values[:, None, :]
    summed = jnp.einsum('bcp,pa->bca', weighted, incidence, precision=lax.Precision.HIGHEST)
    return -summed.reshape(values.shape[0], -1)

def matern(row_desc, col_desc, length):
    inner_prod = jnp.dot(row_desc, col_desc.T, preferred_element_type=jnp.float32)
    row_sq = lax.optimization_barrier(jnp.sum(jnp.square(row_desc.astype(jnp.float32)), axis=1))
    col_sq = lax.optimization_barrier(jnp.sum(jnp.square(col_desc.astype(jnp.float32)), axis=1))
    radius = jnp.sqrt(row_sq[:, None] + col_sq[None, :] - 2.0 * inner_prod) / length
    falloff = jnp.exp(-root_five * radius)
    diag_part = 5.0 / (3.0 * length ** 2) * (1.0 + root_five * radius) * falloff
    outer_part = 25.0 / (3.0 * length ** 4) * falloff
    return (diag_part, outer_part)

def apply_forward(train_desc, induce_desc, diag_part, outer_part, induce_vals):
    self_dot = lax.optimization_barrier(jnp.sum(induce_desc.astype(jnp.float32) * induce_vals.astype(jnp.float32), axis=1))
    projected = jnp.dot(train_desc, induce_vals.T, preferred_element_type=jnp.float32) - self_dot[None, :]
    product = outer_part * projected
    result = jnp.dot(diag_part.astype(jnp.bfloat16), induce_vals, preferred_element_type=jnp.float32)
    result = result + jnp.dot(product.astype(jnp.bfloat16), induce_desc, preferred_element_type=jnp.float32)
    return result - train_desc.astype(jnp.float32) * lax.optimization_barrier(jnp.sum(product, axis=1))[:, None]

def apply_adjoint(train_desc, induce_desc, diag_part, outer_part, train_vals):
    self_dot = lax.optimization_barrier(jnp.sum(train_desc.astype(jnp.float32) * train_vals.astype(jnp.float32), axis=1))
    projected = self_dot[:, None] - jnp.dot(train_vals, induce_desc.T, preferred_element_type=jnp.float32)
    product = outer_part * projected
    result = jnp.dot(diag_part.astype(jnp.bfloat16).T, train_vals, preferred_element_type=jnp.float32)
    result = result - jnp.dot(product.astype(jnp.bfloat16).T, train_desc, preferred_element_type=jnp.float32)
    return result + induce_desc.astype(jnp.float32) * lax.optimization_barrier(jnp.sum(product, axis=0))[:, None]

def reference(train_coords, induce_coords, train_forces, atom_pairs, length_scale):
    atom_count = train_coords.shape[1] // 3
    incidence = make_incidence(atom_pairs, atom_count)
    train_desc, train_grad = centered(train_coords, incidence)
    induce_desc, induce_grad = centered(induce_coords, incidence)
    length = length_scale[0]
    desc_rows = train_desc.reshape(N_TRAIN, TRAIN_DEV, DESC)
    grad_rows = train_grad.reshape(N_TRAIN, TRAIN_DEV, 3, DESC)

    def forward(vectors):
        induce_vals = to_desc(induce_grad, vectors, incidence).astype(jnp.bfloat16)

        def one_section(section):
            desc_sec, grad_sec = section
            diag_part, outer_part = matern(desc_sec, induce_desc, length)
            return to_forces(grad_sec, apply_forward(desc_sec, induce_desc, diag_part, outer_part, induce_vals), incidence)
        return lax.map(one_section, (desc_rows, grad_rows)).reshape(TRAIN_ALL, COMP)

    def adjoint(forces_like):
        train_vals = to_desc(train_grad, forces_like, incidence).astype(jnp.bfloat16).reshape(N_TRAIN, TRAIN_DEV, DESC)

        def add_section(running, section):
            desc_sec, vals_sec = section
            diag_part, outer_part = matern(desc_sec, induce_desc, length)
            return (running + apply_adjoint(desc_sec, induce_desc, diag_part, outer_part, vals_sec), None)
        running, unused = lax.scan(add_section, jnp.zeros((INDUCE_ALL, DESC), jnp.float32), (desc_rows, train_vals))
        return to_forces(induce_grad, running, incidence)
    start = adjoint(train_forces)
    probed = forward(start)
    quotient = jnp.sum(probed * probed) / jnp.sum(train_forces * probed)
    center = 0.775 * quotient
    spread = 0.725 * quotient
    momentum = spread / center
    direction = start / center
    coefficients = direction
    residual = start - adjoint(probed) / center
    for repeat in range(STEPS - 1):
        momentum_next = 1.0 / (2.0 * center / spread - momentum)
        direction = momentum_next * momentum * direction + 2.0 * momentum_next / spread * residual
        coefficients = coefficients + direction
        residual = residual - adjoint(forward(direction))
        momentum = momentum_next
    desc_coeffs = to_desc(induce_grad, coefficients, incidence)
    return (coefficients, residual, desc_coeffs)
```

```python
import functools
import math

import jax
import jax.numpy as jnp
from jax import lax
from jax.experimental import pallas as pl
from jax.experimental.pallas import tpu as pltpu
from jax.sharding import PartitionSpec as P

MESH = pl.DeviceIdType.MESH
F32, BF16 = jnp.float32, jnp.bfloat16
ROOT5 = math.sqrt(5.0)
ATOMS, DESC, PAD = 64, 2016, 2048
NT, NI = 64, 128
TILE = 512
TILES = [pl.ds(j * TILE, TILE) for j in range(PAD // TILE)]
N_TRAIN, N_OWN = 16, 8
OWN0 = 4
N_PLANE, P_OWN = 8, 6
N_ZHI = 4


def dot(a, b):
    return jnp.dot(a, b, preferred_element_type=F32)


def dot_nt(a, b):
    return lax.dot_general(a, b, (((1,), (1,)), ((), ())), preferred_element_type=F32)


def lane_of(shape):
    return lax.broadcasted_iota(jnp.int32, shape, len(shape) - 1)


def pack(wide):
    half = wide.shape[0] // 2
    left = wide[:, 0:128]
    right = jnp.concatenate([wide[:, 128:192], jnp.zeros((wide.shape[0], 64), F32)], axis=1)
    left_turned, right_turned = pltpu.roll(left, 64, 1), pltpu.roll(right, 64, 1)
    low = lane_of((half, 128)) < 64
    return [
        jnp.where(low, left[:half], left_turned[half:]),
        jnp.where(low, left_turned[:half], left[half:]),
        jnp.where(low, right[:half], right_turned[half:]),
    ]


def unpack_into(ref, planes):
    half = planes[0].shape[0]
    low = lane_of((half, 128)) < 64
    turned = [pltpu.roll(p, 64, 1) for p in planes]
    ref[0:half, 0:128] = jnp.where(low, planes[0], turned[1])
    ref[half : 2 * half, 0:128] = jnp.where(low, turned[0], planes[1])
    ref[0:half, 128:192] = planes[2][:, 0:64]
    ref[half : 2 * half, 128:192] = turned[2][:, 0:64]


def two_parts(full):
    high = full.astype(BF16)
    low = (full - high.astype(F32)).astype(BF16)
    return jnp.concatenate([high, low], axis=1)


def spread(planes):
    rows = []
    for plane in planes:
        low = lane_of(plane.shape) < 64
        rows.append(jnp.where(low, plane, 0.0))
        rows.append(jnp.where(low, 0.0, plane))
    return two_parts(jnp.concatenate(rows, axis=0))


def kernel(
    tc, ic, tf, pairs, scale,
    out_coeff, out_resid, out_desc,
    ends, inc, inc_t, grad_t, grad_i, z, vu, vw, desc,
    s_part0, s_part1, s_part2, s_in0, s_in1, s_in2, s_all0, s_all1, s_all2,
    p_part0, p_part1, p_in0, p_in1, p_z0, p_z1, p_all0, p_all1,
    rs_send, rs_recv, ag_send, ag_recv,
    pr_send, pr_recv, pz_send, pz_recv, pg_send, pg_recv, desc_sem,
):
    s_part, s_in, s_all = [s_part0, s_part1, s_part2], [s_in0, s_in1, s_in2], [s_all0, s_all1, s_all2]
    p_part, p_in, p_z, p_all = [p_part0, p_part1], [p_in0, p_in1], [p_z0, p_z1], [p_all0, p_all1]
    t = lax.axis_index("train")
    i = lax.axis_index("induce")
    x, zh, core = i // 8, (i // 2) % 4, i % 2
    spot = x * 2 + core

    def in_plane(other):
        return (t, (other // 2) * 8 + zh * 2 + other % 2)

    def in_column(other):
        return (t, x * 8 + other * 2 + core)

    barrier = pltpu.get_barrier_semaphore()
    for d in range(1, N_TRAIN):
        pl.semaphore_signal(barrier, inc=1, device_id=(lax.rem(t + d, N_TRAIN), i), device_id_type=MESH)
    for d in range(1, N_PLANE):
        pl.semaphore_signal(barrier, inc=1, device_id=in_plane(lax.rem(spot + d, N_PLANE)), device_id_type=MESH)
    for d in range(1, N_ZHI):
        pl.semaphore_signal(barrier, inc=1, device_id=in_column(lax.rem(zh + d, N_ZHI)), device_id_type=MESH)

    ends[...] = jnp.full((2, PAD), -1, jnp.int32)
    ends[:, 0:DESC] = pairs[...]
    atom = lax.rem(lax.broadcasted_iota(jnp.int32, (128, PAD), 0), ATOMS)
    hits = (ends[0:1, :] == atom).astype(F32) - (ends[1:2, :] == atom).astype(F32)
    inc[0:128, :] = hits.astype(BF16)
    inc[128:256, :] = hits.astype(BF16)
    inc_t[...] = hits.T.astype(BF16)

    spot_atom = lax.rem(lane_of((1, 128)), ATOMS)
    lattice = [
        1.5 * lax.rem(spot_atom, 4).astype(F32),
        1.5 * lax.rem(spot_atom // 4, 4).astype(F32),
        1.5 * (spot_atom // 16).astype(F32),
    ]

    def coordinate_rows(planes):
        high, low = [], []
        for plane, points in zip(planes, lattice):
            offset = plane - points
            first = lane_of(plane.shape) < 64
            top = offset.astype(BF16).astype(F32)
            rest = offset - top
            full = jnp.broadcast_to(points, plane.shape)
            high += [jnp.where(first, top, full), jnp.where(first, full, top)]
            low += [jnp.where(first, rest, 0.0), jnp.where(first, 0.0, rest)]
        return jnp.concatenate(
            [jnp.concatenate(high, axis=0).astype(BF16), jnp.concatenate(low, axis=0).astype(BF16)], axis=1
        )

    first8 = lane_of((8, 128)) < 64
    lattice_rows = jnp.concatenate(
        [jnp.where(first8, jnp.broadcast_to(points, (8, 128)), 0.0) for points in lattice], axis=0
    )
    lattice_rows = jnp.concatenate([lattice_rows, jnp.zeros((24, 128), F32)], axis=1).astype(BF16)
    rows_t, rows_i = coordinate_rows(pack(tc[...])), coordinate_rows(pack(ic[...]))

    def describe(rows, tile, last):
        n = rows.shape[0] // 3
        off = dot(rows, inc[:, tile])
        off = [off[0:n], off[n : 2 * n], off[2 * n :]]
        square = off[0] * off[0] + off[1] * off[1] + off[2] * off[2]
        if last:
            square = jnp.where(lane_of(square.shape) < DESC - (PAD - TILE), square, 1.0)
        inverse = lax.rsqrt(square)
        return off, inverse

    for j, tile in enumerate(TILES):
        last = j == len(TILES) - 1
        unused, rest = describe(lattice_rows, tile, last)
        for rows, grad, at, n in ((rows_t, grad_t, 0, NT), (rows_i, grad_i, NT, NI)):
            off, inverse = describe(rows, tile, last)
            cube = -(inverse * inverse * inverse)
            for c in range(3):
                grad[c, :, tile] = off[c] * cube
            z[at : at + n, tile] = (inverse - rest[0:1]).astype(BF16)
    vu[NI:, :] = z[NT:, :]
    vw[NT:, :] = z[0:NT, :]

    length = scale[0]
    gram_t = dot_nt(z[...], z[0:NT, :])
    gram_i = dot_nt(z[...], z[NT:, :])

    def on_diagonal(square, axis):
        rows, columns = square.shape
        same = lax.broadcasted_iota(jnp.int32, (rows, columns), 0) == lane_of((rows, columns))
        return jnp.sum(jnp.where(same, square, 0.0), axis=axis, keepdims=True)

    def matern(inner, row_sq, col_sq):
        radius = jnp.sqrt(jnp.maximum(row_sq + col_sq - 2.0 * inner, 0.0)) / length
        falloff = jnp.exp(-ROOT5 * radius)
        return (
            5.0 / (3.0 * (length * length)) * (1.0 + ROOT5 * radius) * falloff,
            25.0 / (3.0 * (length * length) * (length * length)) * falloff,
        )

    diag, outer = matern(gram_i[0:NT], on_diagonal(gram_t[0:NT], 1), on_diagonal(gram_i[NT:], 0))
    diag_back, outer_back = matern(gram_t[NT:], on_diagonal(gram_i[NT:], 1), on_diagonal(gram_t[0:NT], 0))
    diag = diag.astype(BF16)
    diag_back = jnp.concatenate([diag_back, jnp.zeros((NI, 64), F32)], axis=1)
    outer_back = pltpu.roll(jnp.concatenate([outer_back, jnp.zeros((NI, 64), F32)], axis=1), 64, 1)

    def to_desc(rows, grad, tile):
        n = grad.shape[1]
        moved = dot(rows, inc[:, tile])
        return grad[0, :, tile] * moved[0:n] + grad[1, :, tile] * moved[n : 2 * n] + grad[2, :, tile] * moved[2 * n :]

    def to_forces(values, grad, tile):
        weighted = [(grad[c, :, tile] * values).astype(BF16) for c in range(3)]
        return dot(jnp.concatenate(weighted, axis=0), inc_t[tile, :])

    def packed_planes(total):
        n = total.shape[0] // 3
        low = lane_of((n // 2, 128)) < 64
        return [
            jnp.where(low, total[c * n : c * n + n // 2], total[c * n + n // 2 : (c + 1) * n]) for c in range(3)
        ]

    def forward(planes):
        rows = spread(planes)
        for tile in TILES:
            vu[0:NI, tile] = to_desc(rows, grad_i, tile).astype(BF16)
        gram = dot_nt(z[...], vu[0:NI, :])
        product = outer * (gram[0:NT] - on_diagonal(gram[NT:], 0))
        row_sum = jnp.sum(product, axis=1, keepdims=True)
        both = jnp.concatenate([diag, product.astype(BF16)], axis=1)
        total = jnp.zeros((3 * NT, 128), F32)
        for tile in TILES:
            w = dot(both, vu[:, tile]) - z[0:NT, tile].astype(F32) * row_sum
            total = total + to_forces(w, grad_t, tile)
        return packed_planes(total)

    def adjoint(planes):
        rows = spread(planes)
        for tile in TILES:
            vw[0:NT, tile] = to_desc(rows, grad_t, tile).astype(BF16)
        gram = pltpu.roll(dot_nt(z[...], vw[...]), 64, 1)
        same = lax.broadcasted_iota(jnp.int32, (NT, 128), 0) + 64 == lane_of((NT, 128))
        self_dot = jnp.sum(jnp.where(same, gram[0:NT], 0.0), axis=0, keepdims=True)
        product = outer_back * (self_dot - gram[NT:])
        col_sum = jnp.sum(product, axis=1, keepdims=True)
        both = jnp.where(lane_of((NI, 128)) < 64, diag_back, -product).astype(BF16)
        total = jnp.zeros((3 * NI, 128), F32)
        for tile in TILES:
            h = dot(both, vw[:, tile]) + z[NT:, tile].astype(F32) * col_sum
            total = total + to_forces(h, grad_i, tile)
        return packed_planes(total)

    is_owner = jnp.logical_and(t >= OWN0, t < OWN0 + N_OWN)
    mine = lax.rem(t + N_OWN - OWN0, N_OWN)
    waits = []

    def chunk_rows(k):
        return pl.ds(pl.multiple_of(k * 8, 8), 8)

    def sum_over_train(n, planes, extra=None):
        part, arrived, everything = s_part[n], s_in[n], s_all[n]
        for c in range(3):
            part[c] = planes[c]
        if extra is not None:
            for k in range(N_OWN):
                part[3, k * 8 : (k + 1) * 8, :] = extra

        def scatter(d):
            k = lax.rem(mine + d, N_OWN)
            return pltpu.make_async_remote_copy(
                src_ref=part.at[:, chunk_rows(k), :], dst_ref=arrived.at[t],
                send_sem=rs_send.at[n, d], recv_sem=rs_recv.at[n, t],
                device_id=(k + OWN0, i), device_id_type=MESH,
            )

        def gather(d):
            return pltpu.make_async_remote_copy(
                src_ref=everything.at[:, chunk_rows(mine), :], dst_ref=everything.at[:, chunk_rows(mine), :],
                send_sem=ag_send.at[n, d], recv_sem=ag_recv.at[n, mine],
                device_id=(lax.rem(t + d, N_TRAIN), i), device_id_type=MESH,
            )

        for d in range(1, N_OWN):
            scatter(d).start()

        @pl.when(jnp.logical_not(is_owner))
        def _():
            scatter(0).start()

        @pl.when(is_owner)
        def _():
            total = part[:, chunk_rows(mine), :]
            for d in range(1, N_TRAIN):
                source = lax.rem(t + d, N_TRAIN)
                pltpu.make_async_remote_copy(
                    src_ref=part.at[:, chunk_rows(mine), :], dst_ref=arrived.at[source],
                    send_sem=rs_send.at[n, 0], recv_sem=rs_recv.at[n, source],
                    device_id=(source, i), device_id_type=MESH,
                ).wait_recv()
                total = total + arrived[source]
            everything[:, chunk_rows(mine), :] = total
            for d in range(1, N_TRAIN):
                gather(d).start()

        def arrive():
            for k in range(N_OWN):
                @pl.when(t != k + OWN0)
                def _():
                    rows = pl.ds(k * 8, 8)
                    pltpu.make_async_remote_copy(
                        src_ref=everything.at[:, rows, :], dst_ref=everything.at[:, rows, :],
                        send_sem=ag_send.at[n, 0], recv_sem=ag_recv.at[n, k],
                        device_id=(k + OWN0, i), device_id_type=MESH,
                    ).wait_recv()
            return [everything[c] for c in range(3)]

        def finish():
            for d in range(1, N_OWN):
                scatter(d).wait_send()

            @pl.when(jnp.logical_not(is_owner))
            def _():
                scatter(0).wait_send()

            @pl.when(is_owner)
            def _():
                for d in range(1, N_TRAIN):
                    gather(d).wait_send()

        waits.append(finish)
        return arrive

    has_chunk = spot < P_OWN

    def sum_over_induce(n, planes):
        part, arrived, column, everything = p_part[n], p_in[n], p_z[n], p_all[n]
        for c in range(3):
            for r in range(4):
                part[c * 4 + r] = planes[c][r * 8 : (r + 1) * 8]

        def pair_of(k):
            return pl.ds(k * 2, 2)

        def scatter(d):
            k = lax.rem(spot + d, P_OWN)
            return pltpu.make_async_remote_copy(
                src_ref=part.at[pair_of(k)], dst_ref=arrived.at[spot],
                send_sem=pr_send.at[n, d], recv_sem=pr_recv.at[n, spot],
                device_id=in_plane(k), device_id_type=MESH,
            )

        def across(d):
            return pltpu.make_async_remote_copy(
                src_ref=column.at[zh], dst_ref=column.at[zh],
                send_sem=pz_send.at[n, d], recv_sem=pz_recv.at[n, zh],
                device_id=in_column(lax.rem(zh + d, N_ZHI)), device_id_type=MESH,
            )

        def gather(d):
            return pltpu.make_async_remote_copy(
                src_ref=everything.at[pair_of(spot)], dst_ref=everything.at[pair_of(spot)],
                send_sem=pg_send.at[n, d], recv_sem=pg_recv.at[n, spot],
                device_id=in_plane(lax.rem(spot + d, N_PLANE)), device_id_type=MESH,
            )

        for d in range(1, P_OWN):
            scatter(d).start()

        @pl.when(jnp.logical_not(has_chunk))
        def _():
            scatter(0).start()

        @pl.when(has_chunk)
        def _():
            total = part[pair_of(spot)]
            for d in range(1, N_PLANE):
                source = lax.rem(spot + d, N_PLANE)
                pltpu.make_async_remote_copy(
                    src_ref=part.at[pair_of(spot)], dst_ref=arrived.at[source],
                    send_sem=pr_send.at[n, 0], recv_sem=pr_recv.at[n, source],
                    device_id=in_plane(source), device_id_type=MESH,
                ).wait_recv()
                total = total + arrived[source]
            column[zh] = total
            for d in (2, 1, 3):
                across(d).start()
            for d in range(1, N_ZHI):
                source = lax.rem(zh + d, N_ZHI)
                pltpu.make_async_remote_copy(
                    src_ref=column.at[zh], dst_ref=column.at[source],
                    send_sem=pz_send.at[n, 0], recv_sem=pz_recv.at[n, source],
                    device_id=in_column(source), device_id_type=MESH,
                ).wait_recv()
            everything[pair_of(spot)] = (column[0] + column[1]) + (column[2] + column[3])
            for d in range(1, N_PLANE):
                gather(d).start()

        def arrive():
            for k in range(P_OWN):
                @pl.when(spot != k)
                def _():
                    pltpu.make_async_remote_copy(
                        src_ref=everything.at[pair_of(k)], dst_ref=everything.at[pair_of(k)],
                        send_sem=pg_send.at[n, 0], recv_sem=pg_recv.at[n, k],
                        device_id=in_plane(k), device_id_type=MESH,
                    ).wait_recv()
            return [everything[c * 4 : (c + 1) * 4].reshape(32, 128) for c in range(3)]

        def finish():
            for d in range(1, P_OWN):
                scatter(d).wait_send()

            @pl.when(jnp.logical_not(has_chunk))
            def _():
                scatter(0).wait_send()

            @pl.when(has_chunk)
            def _():
                for d in range(1, N_ZHI):
                    across(d).wait_send()
                for d in range(1, N_PLANE):
                    gather(d).wait_send()

        waits.append(finish)
        return arrive

    def whole_sum(planes, others):
        line = sum(jnp.sum(a * b, axis=0, keepdims=True) for a, b in zip(planes, others))
        return jnp.sum(line, axis=1, keepdims=True)

    forces = pack(tf[...])
    first = adjoint(forces)
    pl.semaphore_wait(barrier, N_TRAIN - 1 + N_PLANE - 1 + N_ZHI - 1)
    start = sum_over_train(0, first)()
    probed = sum_over_induce(0, forward(start))()
    row8 = lax.broadcasted_iota(jnp.int32, (8, 128), 0)
    sums = jnp.where(row8 == 0, whole_sum(probed, probed), whole_sum(forces, probed))
    again = sum_over_train(1, adjoint(probed), sums)()
    quotient = s_all1[3, 0:1, 0:1] / s_all1[3, 1:2, 0:1]
    center = 0.775 * quotient
    spread_ = 0.725 * quotient
    momentum = spread_ / center
    following = 1.0 / (2.0 * center / spread_ - momentum)
    direction = [a / center for a in start]
    residual = [a - b / center for a, b in zip(start, again)]
    turned = [following * momentum * a + 2.0 * following / spread_ * b for a, b in zip(direction, residual)]
    coeffs = [a + b for a, b in zip(direction, turned)]
    arrive = sum_over_induce(1, forward(turned))
    unpack_into(out_coeff, coeffs)
    rows = spread(coeffs)
    for j, tile in enumerate(TILES):
        width = min(TILE, DESC - j * TILE)
        desc[:, pl.ds(j * TILE, width)] = to_desc(rows, grad_i, tile)[:, 0:width]
    copy = pltpu.make_async_copy(desc, out_desc, desc_sem)
    copy.start()
    final = sum_over_train(2, adjoint(arrive()))()
    unpack_into(out_resid, [a - b for a, b in zip(residual, final)])
    for finish in waits:
        finish()
    copy.wait()


def per_device(train_coords, induce_coords, train_forces, atom_pairs, length_scale):
    vmem, dma = pltpu.VMEM, pltpu.SemaphoreType.DMA
    whole = pl.BlockSpec(memory_space=pltpu.VMEM)
    scratch = [
        vmem((2, PAD), jnp.int32), vmem((256, PAD), BF16), vmem((PAD, 128), BF16),
        vmem((3, NT, PAD), F32), vmem((3, NI, PAD), F32),
        vmem((NT + NI, PAD), BF16), vmem((2 * NI, PAD), BF16), vmem((2 * NT, PAD), BF16), vmem((NI, DESC), F32),
    ]
    deep = (3, 4, 3)
    scratch += [vmem((d, 64, 128), F32) for d in deep]
    scratch += [vmem((N_TRAIN, d, 8, 128), F32) for d in deep]
    scratch += [vmem((d, 64, 128), F32) for d in deep]
    scratch += [vmem((12, 8, 128), F32)] * 2
    scratch += [vmem((N_PLANE, 2, 8, 128), F32)] * 2
    scratch += [vmem((N_ZHI, 2, 8, 128), F32)] * 2
    scratch += [vmem((12, 8, 128), F32)] * 2
    scratch += [dma((3, N_OWN)), dma((3, N_TRAIN)), dma((3, N_TRAIN)), dma((3, N_OWN))]
    scratch += [dma((2, N_PLANE)), dma((2, N_PLANE)), dma((2, N_ZHI)), dma((2, N_ZHI)), dma((2, N_PLANE)), dma((2, N_PLANE)), dma]
    return pl.pallas_call(
        kernel,
        out_shape=(
            jax.ShapeDtypeStruct((NI, 192), F32),
            jax.ShapeDtypeStruct((NI, 192), F32),
            jax.ShapeDtypeStruct((NI, DESC), F32),
        ),
        in_specs=[whole, whole, whole, whole, pl.BlockSpec(memory_space=pltpu.SMEM)],
        out_specs=(whole, whole, pl.BlockSpec(memory_space=pl.ANY)),
        scratch_shapes=scratch,
        compiler_params=pltpu.CompilerParams(
            collective_id=0, has_side_effects=True, vmem_limit_bytes=48 * 1024 * 1024
        ),
        cost_estimate=pl.CostEstimate(flops=2_000_000_000, bytes_accessed=2_000_000, transcendentals=1_000_000),
    )(train_coords, induce_coords, train_forces, atom_pairs, length_scale)


def solution(mesh):
    in_specs = (P("train", None), P("induce", None), P("train", None), P(), P())
    out_specs = (P("induce", None), P("induce", None), P("induce", None))
    return jax.shard_map(
        per_device, mesh=mesh, in_specs=in_specs, out_specs=out_specs, check_vma=False
    )
```

```python
import functools
import math

import jax
import jax.numpy as jnp
from jax import lax
from jax.experimental import pallas as pl
from jax.experimental.pallas import tpu as pltpu
from jax.sharding import PartitionSpec as P

MESH = pl.DeviceIdType.MESH
F32, BF16 = jnp.float32, jnp.bfloat16
ROOT5 = math.sqrt(5.0)
ATOMS, DESC, PAD = 64, 2016, 2048
NT, NI = 64, 128
TILE = 1024
DESC_PART = 504
TILES = [pl.ds(j * TILE, TILE) for j in range(PAD // TILE)]
N_TRAIN, N_OWN = 16, 8
OWN0 = 4
N_PLANE, P_OWN = 8, 6
N_ZHI = 4


def dot(a, b):
    return jnp.dot(a, b, preferred_element_type=F32)


def dot_nt(a, b):
    return lax.dot_general(a, b, (((1,), (1,)), ((), ())), preferred_element_type=F32)


def lane_of(shape):
    return lax.broadcasted_iota(jnp.int32, shape, len(shape) - 1)


def pack(wide):
    half = wide.shape[0] // 2
    left = wide[:, 0:128]
    right = wide[:, 128:256]
    if right.shape[1] < 128:
        right = jnp.concatenate([right, jnp.zeros((wide.shape[0], 64), F32)], axis=1)
    left_turned, right_turned = pltpu.roll(left, 64, 1), pltpu.roll(right, 64, 1)
    low = lane_of((half, 128)) < 64
    return [
        jnp.where(low, left[:half], left_turned[half:]),
        jnp.where(low, left_turned[:half], left[half:]),
        jnp.where(low, right[:half], right_turned[half:]),
    ]


def unpack_into(ref, planes):
    for c, plane in enumerate(planes):
        both = jnp.concatenate([plane, pltpu.roll(plane, 64, 1)], axis=0)
        ref[c * ATOMS : (c + 1) * ATOMS, :] = both.T[0:ATOMS]


def two_parts(full):
    high = full.astype(BF16)
    low = (full - high.astype(F32)).astype(BF16)
    return jnp.concatenate([high, low], axis=1)


def spread(planes):
    rows = []
    for plane in planes:
        low = lane_of(plane.shape) < 64
        rows.append(jnp.where(low, plane, 0.0))
        rows.append(jnp.where(low, 0.0, plane))
    return two_parts(jnp.concatenate(rows, axis=0))


def kernel(
    tc_far, ic_far, tf_far, pairs_far, scale,
    far_coeff, far_resid, far_desc,
    out_coeff, out_resid, out_desc,
    tc, ic, tf, pairs, ends, inc, inc_t, grad_t, grad_i, z, vu, vw,
    s_part0, s_part1, s_part2, s_in0, s_in1, s_in2, s_all0, s_all1, s_all2,
    p_part0, p_part1, p_in0, p_in1, p_z0, p_z1, p_all0, p_all1,
    rs_send, rs_recv, ag_send, ag_recv,
    pr_send, pr_recv, pz_send, pz_recv, pg_send, pg_recv, load_sem, store_sem,
):
    s_part, s_in, s_all = [s_part0, s_part1, s_part2], [s_in0, s_in1, s_in2], [s_all0, s_all1, s_all2]
    p_part, p_in, p_z, p_all = [p_part0, p_part1], [p_in0, p_in1], [p_z0, p_z1], [p_all0, p_all1]
    t = lax.axis_index("train")
    i = lax.axis_index("induce")
    x, zh, core = i // 8, (i // 2) % 4, i % 2
    spot = x * 2 + core

    def in_plane(other):
        return (t, (other // 2) * 8 + zh * 2 + other % 2)

    def in_column(other):
        return (t, x * 8 + other * 2 + core)

    loads = [
        pltpu.make_async_copy(source, target, load_sem.at[k])
        for k, (source, target) in enumerate(((pairs_far, pairs), (ic_far, ic), (tc_far, tc), (tf_far, tf)))
    ]
    for load in loads:
        load.start()

    barrier = pltpu.get_barrier_semaphore()
    for d in range(1, N_TRAIN):
        pl.semaphore_signal(barrier, inc=1, device_id=(lax.rem(t + d, N_TRAIN), i), device_id_type=MESH)
    for d in range(1, N_PLANE):
        pl.semaphore_signal(barrier, inc=1, device_id=in_plane(lax.rem(spot + d, N_PLANE)), device_id_type=MESH)
    for d in range(1, N_ZHI):
        pl.semaphore_signal(barrier, inc=1, device_id=in_column(lax.rem(zh + d, N_ZHI)), device_id_type=MESH)

    for load in loads:
        load.wait()

    ends[...] = jnp.full((2, PAD), -1, jnp.int32)
    ends[:, 0:DESC] = pairs[...]
    atom = lax.rem(lax.broadcasted_iota(jnp.int32, (128, PAD), 0), ATOMS)
    hits = (ends[0:1, :] == atom).astype(F32) - (ends[1:2, :] == atom).astype(F32)
    inc[0:128, :] = hits.astype(BF16)
    inc[128:256, :] = hits.astype(BF16)
    inc_t[...] = hits.T.astype(BF16)

    spot_atom = lax.rem(lane_of((1, 128)), ATOMS)
    lattice = [
        1.5 * lax.rem(spot_atom, 4).astype(F32),
        1.5 * lax.rem(spot_atom // 4, 4).astype(F32),
        1.5 * (spot_atom // 16).astype(F32),
    ]

    def coordinate_rows(planes):
        high, low = [], []
        for plane, points in zip(planes, lattice):
            offset = plane - points
            first = lane_of(plane.shape) < 64
            top = offset.astype(BF16).astype(F32)
            rest = offset - top
            full = jnp.broadcast_to(points, plane.shape)
            high += [jnp.where(first, top, full), jnp.where(first, full, top)]
            low += [jnp.where(first, rest, 0.0), jnp.where(first, 0.0, rest)]
        return jnp.concatenate(
            [jnp.concatenate(high, axis=0).astype(BF16), jnp.concatenate(low, axis=0).astype(BF16)], axis=1
        )

    first8 = lane_of((8, 128)) < 64
    lattice_rows = jnp.concatenate(
        [jnp.where(first8, jnp.broadcast_to(points, (8, 128)), 0.0) for points in lattice], axis=0
    )
    lattice_rows = jnp.concatenate([lattice_rows, jnp.zeros((24, 128), F32)], axis=1).astype(BF16)
    rows_t, rows_i = coordinate_rows(pack(tc[...])), coordinate_rows(pack(jnp.concatenate([ic[...], jnp.zeros((64, NI), F32)], axis=0).T))

    def describe(rows, tile, last):
        n = rows.shape[0] // 3
        off = dot(rows, inc[:, tile])
        off = [off[0:n], off[n : 2 * n], off[2 * n :]]
        square = off[0] * off[0] + off[1] * off[1] + off[2] * off[2]
        if last:
            square = jnp.where(lane_of(square.shape) < DESC - (PAD - TILE), square, 1.0)
        inverse = lax.rsqrt(square)
        return off, inverse

    for j, tile in enumerate(TILES):
        last = j == len(TILES) - 1
        unused, rest = describe(lattice_rows, tile, last)
        for rows, grad, at, n in ((rows_t, grad_t, 0, NT), (rows_i, grad_i, NT, NI)):
            off, inverse = describe(rows, tile, last)
            cube = -(inverse * inverse * inverse)
            for c in range(3):
                grad[c, :, tile] = off[c] * cube
            z[at : at + n, tile] = (inverse - rest[0:1]).astype(BF16)
    vu[NI:, :] = z[NT:, :]
    vw[NT:, :] = z[0:NT, :]

    length = scale[0]
    gram_t = dot_nt(z[...], z[0:NT, :])
    gram_i = dot_nt(z[...], z[NT:, :])

    def on_diagonal(square, axis):
        rows, columns = square.shape
        same = lax.broadcasted_iota(jnp.int32, (rows, columns), 0) == lane_of((rows, columns))
        return jnp.sum(jnp.where(same, square, 0.0), axis=axis, keepdims=True)

    def matern(inner, row_sq, col_sq):
        radius = jnp.sqrt(jnp.maximum(row_sq + col_sq - 2.0 * inner, 0.0)) / length
        falloff = jnp.exp(-ROOT5 * radius)
        return (
            5.0 / (3.0 * (length * length)) * (1.0 + ROOT5 * radius) * falloff,
            25.0 / (3.0 * (length * length) * (length * length)) * falloff,
        )

    diag, outer = matern(gram_i[0:NT], on_diagonal(gram_t[0:NT], 1), on_diagonal(gram_i[NT:], 0))
    diag_back, outer_back = matern(gram_t[NT:], on_diagonal(gram_i[NT:], 1), on_diagonal(gram_t[0:NT], 0))
    diag = diag.astype(BF16)
    diag_back = jnp.concatenate([diag_back, jnp.zeros((NI, 64), F32)], axis=1)
    outer_back = pltpu.roll(jnp.concatenate([outer_back, jnp.zeros((NI, 64), F32)], axis=1), 64, 1)

    def to_desc(rows, grad, tile):
        n = grad.shape[1]
        moved = dot(rows, inc[:, tile])
        return grad[0, :, tile] * moved[0:n] + grad[1, :, tile] * moved[n : 2 * n] + grad[2, :, tile] * moved[2 * n :]

    def to_forces(values, grad, tile):
        weighted = [(grad[c, :, tile] * values).astype(BF16) for c in range(3)]
        return dot(jnp.concatenate(weighted, axis=0), inc_t[tile, :])

    def packed_planes(total):
        n = total.shape[0] // 3
        low = lane_of((n // 2, 128)) < 64
        return [
            jnp.where(low, total[c * n : c * n + n // 2], total[c * n + n // 2 : (c + 1) * n]) for c in range(3)
        ]

    def forward(planes):
        rows = spread(planes)
        for tile in TILES:
            vu[0:NI, tile] = to_desc(rows, grad_i, tile).astype(BF16)
        gram = dot_nt(z[...], vu[0:NI, :])
        product = outer * (gram[0:NT] - on_diagonal(gram[NT:], 0))
        row_sum = jnp.sum(product, axis=1, keepdims=True)
        both = jnp.concatenate([diag, product.astype(BF16)], axis=1)
        total = jnp.zeros((3 * NT, 128), F32)
        for tile in TILES:
            w = dot(both, vu[:, tile]) - z[0:NT, tile].astype(F32) * row_sum
            total = total + to_forces(w, grad_t, tile)
        return packed_planes(total)

    def adjoint(planes):
        rows = spread(planes)
        for tile in TILES:
            vw[0:NT, tile] = to_desc(rows, grad_t, tile).astype(BF16)
        gram = pltpu.roll(dot_nt(z[...], vw[...]), 64, 1)
        same = lax.broadcasted_iota(jnp.int32, (NT, 128), 0) + 64 == lane_of((NT, 128))
        self_dot = jnp.sum(jnp.where(same, gram[0:NT], 0.0), axis=0, keepdims=True)
        product = outer_back * (self_dot - gram[NT:])
        col_sum = jnp.sum(product, axis=1, keepdims=True)
        both = jnp.where(lane_of((NI, 128)) < 64, diag_back, -product).astype(BF16)
        total = jnp.zeros((3 * NI, 128), F32)
        for tile in TILES:
            h = dot(both, vw[:, tile]) + z[NT:, tile].astype(F32) * col_sum
            total = total + to_forces(h, grad_i, tile)
        return packed_planes(total)

    z_lo, y = t // 4, lax.rem(t, 4)
    is_owner = jnp.logical_or(z_lo == 1, z_lo == 2)
    mine = lax.rem(t + N_OWN - OWN0, N_OWN)
    far = jnp.where(z_lo <= 1, 2, 1)
    near = 3 - far
    to_owners = [(far, 2), (near, 2), (far, 1), (far, 3), (near, 1), (near, 3), (far, 0), (near, 0)]
    end = jnp.where(z_lo == 1, 3, 0)
    inner, edge = 3 - z_lo, 3 - end
    to_all = [
        (end, 2), (end, 1), (end, 3), (inner, 2), (edge, 2), (end, 0), (inner, 1), (inner, 3),
        (edge, 1), (edge, 3), (z_lo, 2), (inner, 0), (edge, 0), (z_lo, 1), (z_lo, 3),
    ]
    waits = []

    def spot_of(step):
        return step[0] * 4 + lax.rem(y + step[1], 4)

    def chunk_rows(k):
        return pl.ds(pl.multiple_of(k * 8, 8), 8)

    def drain():
        while waits:
            waits.pop(0)()

    def sum_over_train(n, planes, extra=None):
        part, arrived, everything = s_part[n], s_in[n], s_all[n]
        for c in range(3):
            part[c] = planes[c]
        if extra is not None:
            for k in range(N_OWN):
                part[3, k * 8 : (k + 1) * 8, :] = extra

        def scatter(d):
            owner = spot_of(to_owners[d])
            return pltpu.make_async_remote_copy(
                src_ref=part.at[:, chunk_rows(owner - OWN0), :], dst_ref=arrived.at[t],
                send_sem=rs_send.at[n, d], recv_sem=rs_recv.at[n, t],
                device_id=(owner, i), device_id_type=MESH,
            )

        def gather(d):
            return pltpu.make_async_remote_copy(
                src_ref=everything.at[:, chunk_rows(mine), :], dst_ref=everything.at[:, chunk_rows(mine), :],
                send_sem=ag_send.at[n, d], recv_sem=ag_recv.at[n, mine],
                device_id=(spot_of(to_all[d]), i), device_id_type=MESH,
            )

        for d in range(N_OWN - 1):
            scatter(d).start()

        @pl.when(jnp.logical_not(is_owner))
        def _():
            scatter(N_OWN - 1).start()

        drain()

        @pl.when(is_owner)
        def _():
            total = part[:, chunk_rows(mine), :]
            for step in reversed(to_all):
                source = spot_of(step)
                pltpu.make_async_remote_copy(
                    src_ref=part.at[:, chunk_rows(mine), :], dst_ref=arrived.at[source],
                    send_sem=rs_send.at[n, 0], recv_sem=rs_recv.at[n, source],
                    device_id=(source, i), device_id_type=MESH,
                ).wait_recv()
                total = total + arrived[source]
            everything[:, chunk_rows(mine), :] = total
            for d in range(N_TRAIN - 1):
                gather(d).start()

        def arrive():
            for k in range(N_OWN):
                @pl.when(t != k + OWN0)
                def _():
                    rows = pl.ds(k * 8, 8)
                    pltpu.make_async_remote_copy(
                        src_ref=everything.at[:, rows, :], dst_ref=everything.at[:, rows, :],
                        send_sem=ag_send.at[n, 0], recv_sem=ag_recv.at[n, k],
                        device_id=(k + OWN0, i), device_id_type=MESH,
                    ).wait_recv()
            return [everything[c] for c in range(3)]

        def finish():
            for d in range(N_OWN - 1):
                scatter(d).wait_send()

            @pl.when(jnp.logical_not(is_owner))
            def _():
                scatter(N_OWN - 1).wait_send()

            @pl.when(is_owner)
            def _():
                for d in range(N_TRAIN - 1):
                    gather(d).wait_send()

        waits.append(finish)
        return arrive

    has_chunk = x < P_OWN // 2
    in_plane_steps = [(2, 0), (2, 1), (1, 0), (3, 0), (1, 1), (3, 1), (0, 1)]

    def plane_spot(step):
        return lax.rem(x + step[0], 4) * 2 + lax.rem(core + step[1], 2)

    def sum_over_induce(n, planes):
        part, arrived, column, everything = p_part[n], p_in[n], p_z[n], p_all[n]
        for c in range(3):
            for r in range(4):
                part[c * 4 + r] = planes[c][r * 8 : (r + 1) * 8]

        def pair_of(k):
            return pl.ds(k * 2, 2)

        def scatter(d):
            k = plane_spot(in_plane_steps[d])
            return pltpu.make_async_remote_copy(
                src_ref=part.at[pair_of(k)], dst_ref=arrived.at[spot],
                send_sem=pr_send.at[n, d], recv_sem=pr_recv.at[n, spot],
                device_id=in_plane(k), device_id_type=MESH,
            )

        def across(d):
            return pltpu.make_async_remote_copy(
                src_ref=column.at[zh], dst_ref=column.at[zh],
                send_sem=pz_send.at[n, d], recv_sem=pz_recv.at[n, zh],
                device_id=in_column(lax.rem(zh + d, N_ZHI)), device_id_type=MESH,
            )

        def gather(d):
            return pltpu.make_async_remote_copy(
                src_ref=everything.at[pair_of(spot)], dst_ref=everything.at[pair_of(spot)],
                send_sem=pg_send.at[n, d], recv_sem=pg_recv.at[n, spot],
                device_id=in_plane(plane_spot(in_plane_steps[d])), device_id_type=MESH,
            )

        def for_owners(act):
            for d, step in enumerate(in_plane_steps):
                @pl.when(plane_spot(step) < P_OWN)
                def _():
                    act(d)

        for_owners(lambda d: scatter(d).start())
        drain()

        @pl.when(has_chunk)
        def _():
            total = part[pair_of(spot)]
            for step in reversed(in_plane_steps):
                source = plane_spot(step)
                pltpu.make_async_remote_copy(
                    src_ref=part.at[pair_of(spot)], dst_ref=arrived.at[source],
                    send_sem=pr_send.at[n, 0], recv_sem=pr_recv.at[n, source],
                    device_id=in_plane(source), device_id_type=MESH,
                ).wait_recv()
                total = total + arrived[source]
            column[zh] = total
            for d in (2, 1, 3):
                across(d).start()
            for d in (1, 3, 2):
                source = lax.rem(zh + d, N_ZHI)
                pltpu.make_async_remote_copy(
                    src_ref=column.at[zh], dst_ref=column.at[source],
                    send_sem=pz_send.at[n, 0], recv_sem=pz_recv.at[n, source],
                    device_id=in_column(source), device_id_type=MESH,
                ).wait_recv()
            everything[pair_of(spot)] = (column[0] + column[1]) + (column[2] + column[3])
            for d in range(N_PLANE - 1):
                gather(d).start()

        def arrived_from(d):
            k = plane_spot(in_plane_steps[d])
            pltpu.make_async_remote_copy(
                src_ref=everything.at[pair_of(k)], dst_ref=everything.at[pair_of(k)],
                send_sem=pg_send.at[n, 0], recv_sem=pg_recv.at[n, k],
                device_id=in_plane(k), device_id_type=MESH,
            ).wait_recv()

        def arrive():
            for_owners(arrived_from)
            return [everything[c * 4 : (c + 1) * 4].reshape(32, 128) for c in range(3)]

        def finish():
            for_owners(lambda d: scatter(d).wait_send())

            @pl.when(has_chunk)
            def _():
                for d in range(1, N_ZHI):
                    across(d).wait_send()
                for d in range(N_PLANE - 1):
                    gather(d).wait_send()

        waits.append(finish)
        return arrive

    def whole_sum(planes, others):
        line = sum(jnp.sum(a * b, axis=0, keepdims=True) for a, b in zip(planes, others))
        return jnp.sum(line, axis=1, keepdims=True)

    forces = pack(tf[...])
    first = adjoint(forces)
    pl.semaphore_wait(barrier, N_TRAIN - 1 + N_PLANE - 1 + N_ZHI - 1)
    start = sum_over_train(0, first)()
    probed = sum_over_induce(0, forward(start))()
    row8 = lax.broadcasted_iota(jnp.int32, (8, 128), 0)
    sums = jnp.where(row8 == 0, whole_sum(probed, probed), whole_sum(forces, probed))
    again = sum_over_train(1, adjoint(probed), sums)()
    quotient = s_all1[3, 0:1, 0:1] / s_all1[3, 1:2, 0:1]
    center = 0.775 * quotient
    spread_ = 0.725 * quotient
    momentum = spread_ / center
    following = 1.0 / (2.0 * center / spread_ - momentum)
    direction = [a / center for a in start]
    residual = [a - b / center for a, b in zip(start, again)]
    turned = [following * momentum * a + 2.0 * following / spread_ * b for a, b in zip(direction, residual)]
    coeffs = [a + b for a, b in zip(direction, turned)]
    arrive = sum_over_induce(1, forward(turned))
    unpack_into(out_coeff, coeffs)
    rows = spread(coeffs)
    for j, tile in enumerate(TILES):
        width = min(TILE, DESC - j * TILE)
        out_desc[pl.ds(j * TILE, width), :] = to_desc(rows, grad_i, tile).T[0:width]
    stores = [
        pltpu.make_async_copy(source, target, store_sem.at[k])
        for k, (source, target) in enumerate(((out_desc, far_desc), (out_coeff, far_coeff), (out_resid, far_resid)))
    ]
    stores[0].start()
    stores[1].start()
    final = sum_over_train(2, adjoint(arrive()))()
    unpack_into(out_resid, [a - b for a, b in zip(residual, final)])
    stores[2].start()
    drain()
    for store in stores:
        store.wait()


def write_out(coeffs, resid, desc, out_coeffs, out_resid, out_desc, via_coeffs, via_resid, via_desc, in_sem, out_sem):
    parts = [(desc, via_desc, out_desc, k * DESC_PART, DESC_PART) for k in range(DESC // DESC_PART)]
    parts += [(coeffs, via_coeffs, out_coeffs, 0, 192), (resid, via_resid, out_resid, 0, 192)]
    ins, outs = [], []
    for k, (source, via, target, at, size) in enumerate(parts):
        rows = pl.ds(at, size)
        ins.append(pltpu.make_async_copy(source.at[rows], via.at[rows], in_sem.at[k]))
        outs.append(pltpu.make_async_copy(via.at[rows], target.at[rows], out_sem.at[k]))
    for copy in ins:
        copy.start()
    for first, second in zip(ins, outs):
        first.wait()
        second.start()
    for copy in outs:
        copy.wait()


def per_device(train_coords, induce_coords, train_forces, atom_pairs, length_scale):
    vmem, dma = pltpu.VMEM, pltpu.SemaphoreType.DMA
    whole = pl.BlockSpec(memory_space=pltpu.VMEM)
    scratch = [vmem((192, NI), F32), vmem((192, NI), F32), vmem((DESC, NI), F32)]
    scratch += [
        vmem((NT, 192), F32), vmem((192, NI), F32), vmem((NT, 192), F32), vmem((2, DESC), jnp.int32),
        vmem((2, PAD), jnp.int32), vmem((256, PAD), BF16), vmem((PAD, 128), BF16),
        vmem((3, NT, PAD), F32), vmem((3, NI, PAD), F32),
        vmem((NT + NI, PAD), BF16), vmem((2 * NI, PAD), BF16), vmem((2 * NT, PAD), BF16),
    ]
    deep = (3, 4, 3)
    scratch += [vmem((d, 64, 128), F32) for d in deep]
    scratch += [vmem((N_TRAIN, d, 8, 128), F32) for d in deep]
    scratch += [vmem((d, 64, 128), F32) for d in deep]
    scratch += [vmem((12, 8, 128), F32)] * 2
    scratch += [vmem((N_PLANE, 2, 8, 128), F32)] * 2
    scratch += [vmem((N_ZHI, 2, 8, 128), F32)] * 2
    scratch += [vmem((12, 8, 128), F32)] * 2
    scratch += [dma((3, N_OWN)), dma((3, N_TRAIN)), dma((3, N_TRAIN)), dma((3, N_OWN))]
    scratch += [dma((2, N_PLANE)), dma((2, N_PLANE)), dma((2, N_ZHI)), dma((2, N_ZHI)), dma((2, N_PLANE)), dma((2, N_PLANE)), dma((4,)), dma((3,))]
    results = pl.pallas_call(
        kernel,
        out_shape=(
            jax.ShapeDtypeStruct((192, NI), F32),
            jax.ShapeDtypeStruct((192, NI), F32),
            jax.ShapeDtypeStruct((DESC, NI), F32),
        ),
        in_specs=[pl.BlockSpec(memory_space=pltpu.HBM)] * 4 + [pl.BlockSpec(memory_space=pltpu.SMEM)],
        out_specs=(pl.BlockSpec(memory_space=pltpu.HBM),) * 3,
        scratch_shapes=scratch,
        compiler_params=pltpu.CompilerParams(
            collective_id=0, has_side_effects=True, vmem_limit_bytes=63 * 1024 * 1024
        ),
        cost_estimate=pl.CostEstimate(flops=2_000_000_000, bytes_accessed=2_000_000, transcendentals=1_000_000),
    )(train_coords, induce_coords.T, train_forces, atom_pairs, length_scale)
    coeffs, resid, desc = pl.pallas_call(
        write_out,
        out_shape=[jax.ShapeDtypeStruct(r.shape, r.dtype) for r in results],
        in_specs=[pl.BlockSpec(memory_space=pltpu.HBM)] * 3,
        out_specs=[pl.BlockSpec(memory_space=pltpu.HBM)] * 3,
        scratch_shapes=[vmem(r.shape, r.dtype) for r in results] + [dma((DESC // DESC_PART + 2,))] * 2,
    )(*results)
    return coeffs.T, resid.T, desc.T


def solution(mesh):
    in_specs = (P("train", None), P("induce", None), P("train", None), P(), P())
    out_specs = (P("induce", None), P("induce", None), P("induce", None))
    return jax.shard_map(
        per_device, mesh=mesh, in_specs=in_specs, out_specs=out_specs, check_vma=False
    )
```

```python
import functools
import math

import jax
import jax.numpy as jnp
from jax import lax
from jax.experimental import pallas as pl
from jax.experimental.pallas import tpu as pltpu
from jax.sharding import PartitionSpec as P

MESH = pl.DeviceIdType.MESH
F32, BF16 = jnp.float32, jnp.bfloat16
ROOT5 = math.sqrt(5.0)
ATOMS, DESC, PAD = 64, 2016, 2048
NT, NI = 64, 128
TILE = 1024
DESC_PART = 504
TILES = [pl.ds(j * TILE, TILE) for j in range(PAD // TILE)]
N_TRAIN, N_OWN = 16, 8
OWN0 = 4
N_PLANE, P_OWN = 8, 6
N_ZHI = 4


def dot(a, b):
    return jnp.dot(a, b, preferred_element_type=F32)


def dot_nt(a, b):
    return lax.dot_general(a, b, (((1,), (1,)), ((), ())), preferred_element_type=F32)


def lane_of(shape):
    return lax.broadcasted_iota(jnp.int32, shape, len(shape) - 1)


def pack(wide):
    half = wide.shape[0] // 2
    left = wide[:, 0:128]
    right = wide[:, 128:256]
    if right.shape[1] < 128:
        right = jnp.concatenate([right, jnp.zeros((wide.shape[0], 64), F32)], axis=1)
    left_turned, right_turned = pltpu.roll(left, 64, 1), pltpu.roll(right, 64, 1)
    low = lane_of((half, 128)) < 64
    return [
        jnp.where(low, left[:half], left_turned[half:]),
        jnp.where(low, left_turned[:half], left[half:]),
        jnp.where(low, right[:half], right_turned[half:]),
    ]


def unpack_into(ref, planes):
    for c, plane in enumerate(planes):
        both = jnp.concatenate([plane, pltpu.roll(plane, 64, 1)], axis=0)
        ref[c * ATOMS : (c + 1) * ATOMS, :] = both.T[0:ATOMS]


def two_parts(full):
    high = full.astype(BF16)
    low = (full - high.astype(F32)).astype(BF16)
    return jnp.concatenate([high, low], axis=1)


def spread(planes):
    rows = []
    for plane in planes:
        low = lane_of(plane.shape) < 64
        rows.append(jnp.where(low, plane, 0.0))
        rows.append(jnp.where(low, 0.0, plane))
    return two_parts(jnp.concatenate(rows, axis=0))


def kernel(
    tc_far, ic_far, tf_far, pairs_far, scale,
    far_coeff, far_resid, far_desc,
    out_coeff, out_resid, out_desc,
    tc, ic, tf, pairs, ends, inc, inc_t, grad_t, grad_i, z, vu, vw, diag_ref, outer_ref, both_ref, sum_ref,
    s_part0, s_part1, s_part2, s_in0, s_in1, s_in2, s_all0, s_all1, s_all2,
    p_part0, p_part1, p_in0, p_in1, p_z0, p_z1, p_all0, p_all1,
    rs_send, rs_recv, ag_send, ag_recv,
    pr_send, pr_recv, pz_send, pz_recv, pg_send, pg_recv, load_sem, store_sem,
):
    s_part, s_in, s_all = [s_part0, s_part1, s_part2], [s_in0, s_in1, s_in2], [s_all0, s_all1, s_all2]
    p_part, p_in, p_z, p_all = [p_part0, p_part1], [p_in0, p_in1], [p_z0, p_z1], [p_all0, p_all1]
    t = lax.axis_index("train")
    i = lax.axis_index("induce")
    x, zh, core = i // 8, (i // 2) % 4, i % 2
    spot = x * 2 + core

    def in_plane(other):
        return (t, (other // 2) * 8 + zh * 2 + other % 2)

    def in_column(other):
        return (t, x * 8 + other * 2 + core)

    barrier = pltpu.get_barrier_semaphore()
    for d in (2, 1, 3):
        pl.semaphore_signal(barrier, inc=1, device_id=in_column(lax.rem(zh + d, N_ZHI)), device_id_type=MESH)
    loads = [
        pltpu.make_async_copy(source, target, load_sem.at[k])
        for k, (source, target) in enumerate(((pairs_far, pairs), (ic_far, ic), (tc_far, tc), (tf_far, tf)))
    ]
    for load in loads:
        load.start()

    for d in range(1, N_TRAIN):
        pl.semaphore_signal(barrier, inc=1, device_id=(lax.rem(t + d, N_TRAIN), i), device_id_type=MESH)
    for d in range(1, N_PLANE):
        pl.semaphore_signal(barrier, inc=1, device_id=in_plane(lax.rem(spot + d, N_PLANE)), device_id_type=MESH)

    for load in loads:
        load.wait()

    ends[...] = jnp.full((2, PAD), -1, jnp.int32)
    ends[:, 0:DESC] = pairs[...]
    atom = lax.rem(lax.broadcasted_iota(jnp.int32, (128, PAD), 0), ATOMS)
    hits = (ends[0:1, :] == atom).astype(F32) - (ends[1:2, :] == atom).astype(F32)
    inc[0:128, :] = hits.astype(BF16)
    inc[128:256, :] = hits.astype(BF16)
    inc_t[...] = hits.T.astype(BF16)

    spot_atom = lax.rem(lane_of((1, 128)), ATOMS)
    lattice = [
        1.5 * lax.rem(spot_atom, 4).astype(F32),
        1.5 * lax.rem(spot_atom // 4, 4).astype(F32),
        1.5 * (spot_atom // 16).astype(F32),
    ]

    def coordinate_rows(planes):
        high, low = [], []
        for plane, points in zip(planes, lattice):
            offset = plane - points
            first = lane_of(plane.shape) < 64
            top = offset.astype(BF16).astype(F32)
            rest = offset - top
            full = jnp.broadcast_to(points, plane.shape)
            high += [jnp.where(first, top, full), jnp.where(first, full, top)]
            low += [jnp.where(first, rest, 0.0), jnp.where(first, 0.0, rest)]
        return jnp.concatenate(
            [jnp.concatenate(high, axis=0).astype(BF16), jnp.concatenate(low, axis=0).astype(BF16)], axis=1
        )

    first8 = lane_of((8, 128)) < 64
    lattice_rows = jnp.concatenate(
        [jnp.where(first8, jnp.broadcast_to(points, (8, 128)), 0.0) for points in lattice], axis=0
    )
    lattice_rows = jnp.concatenate([lattice_rows, jnp.zeros((24, 128), F32)], axis=1).astype(BF16)
    rows_t, rows_i = coordinate_rows(pack(tc[...])), coordinate_rows(pack(jnp.concatenate([ic[...], jnp.zeros((64, NI), F32)], axis=0).T))

    def describe(rows, tile, last):
        n = rows.shape[0] // 3
        off = dot(rows, inc[:, tile])
        off = [off[0:n], off[n : 2 * n], off[2 * n :]]
        square = off[0] * off[0] + off[1] * off[1] + off[2] * off[2]
        if last:
            square = jnp.where(lane_of(square.shape) < DESC - (PAD - TILE), square, 1.0)
        inverse = lax.rsqrt(square)
        return off, inverse

    for j, tile in enumerate(TILES):
        last = j == len(TILES) - 1
        unused, rest = describe(lattice_rows, tile, last)
        for rows, grad, at, n in ((rows_t, grad_t, 0, NT), (rows_i, grad_i, NT, NI)):
            off, inverse = describe(rows, tile, last)
            cube = -(inverse * inverse * inverse)
            for c in range(3):
                grad[c, :, tile] = off[c] * cube
            z[at : at + n, tile] = (inverse - rest[0:1]).astype(BF16)
    vw[NT:, :] = z[0:NT, :]

    length = scale[0]
    gram_t = dot_nt(z[...], z[0:NT, :])
    gram_i = dot_nt(z[NT:, :], z[NT:, :])

    def on_diagonal(square, axis):
        rows, columns = square.shape
        same = lax.broadcasted_iota(jnp.int32, (rows, columns), 0) == lane_of((rows, columns))
        return jnp.sum(jnp.where(same, square, 0.0), axis=axis, keepdims=True)

    def matern(inner, row_sq, col_sq):
        radius = jnp.sqrt(jnp.maximum(row_sq + col_sq - 2.0 * inner, 0.0)) / length
        falloff = jnp.exp(-ROOT5 * radius)
        return (
            5.0 / (3.0 * (length * length)) * (1.0 + ROOT5 * radius) * falloff,
            25.0 / (3.0 * (length * length) * (length * length)) * falloff,
        )

    diag_back, outer_back = matern(gram_t[NT:], on_diagonal(gram_i, 1), on_diagonal(gram_t[0:NT], 0))
    diag_back = jnp.concatenate([diag_back, jnp.zeros((NI, 64), F32)], axis=1)
    outer_back = pltpu.roll(jnp.concatenate([outer_back, jnp.zeros((NI, 64), F32)], axis=1), 64, 1)

    def to_desc(rows, grad, tile):
        n = grad.shape[1]
        moved = dot(rows, inc[:, tile])
        return grad[0, :, tile] * moved[0:n] + grad[1, :, tile] * moved[n : 2 * n] + grad[2, :, tile] * moved[2 * n :]

    def to_forces(values, grad, tile):
        weighted = [(grad[c, :, tile] * values).astype(BF16) for c in range(3)]
        return dot(jnp.concatenate(weighted, axis=0), inc_t[tile, :])

    def packed_planes(total):
        n = total.shape[0] // 3
        low = lane_of((n // 2, 128)) < 64
        return [
            jnp.where(low, total[c * n : c * n + n // 2], total[c * n + n // 2 : (c + 1) * n]) for c in range(3)
        ]

    def forward(planes):
        rows = spread(planes)
        for tile in TILES:
            vu[0:NI, tile] = to_desc(rows, grad_i, tile).astype(BF16)
        gram = dot_nt(z[...], vu[0:NI, :])
        product = outer_ref[...] * (gram[0:NT] - on_diagonal(gram[NT:], 0))
        row_sum = jnp.sum(product, axis=1, keepdims=True)
        both = jnp.concatenate([diag_ref[...], product.astype(BF16)], axis=1)
        total = jnp.zeros((3 * NT, 128), F32)
        for tile in TILES:
            w = dot(both, vu[:, tile]) - z[0:NT, tile].astype(F32) * row_sum
            total = total + to_forces(w, grad_t, tile)
        return packed_planes(total)

    def adjoint(planes):
        rows = spread(planes)
        for tile in TILES:
            vw[0:NT, tile] = to_desc(rows, grad_t, tile).astype(BF16)
        gram = pltpu.roll(dot_nt(z[...], vw[...]), 64, 1)
        same = lax.broadcasted_iota(jnp.int32, (NT, 128), 0) + 64 == lane_of((NT, 128))
        self_dot = jnp.sum(jnp.where(same, gram[0:NT], 0.0), axis=0, keepdims=True)
        product = outer_back * (self_dot - gram[NT:])
        col_sum = jnp.sum(product, axis=1, keepdims=True)
        both = jnp.where(lane_of((NI, 128)) < 64, diag_back, -product).astype(BF16)
        both_ref[...] = both
        sum_ref[...] = jnp.broadcast_to(col_sum, (NI, 128))

    def adjoint_half(plane):
        at = pl.multiple_of(plane * 32, 32)
        low, high = pl.ds(at, 32), pl.ds(at + 64, 32)
        both = jnp.concatenate([both_ref[low, :], both_ref[high, :]], axis=0)
        col_sum = jnp.concatenate([sum_ref[low, :], sum_ref[high, :]], axis=0)[:, 0:1]
        total = jnp.zeros((3 * 64, 128), F32)
        for tile in TILES:
            own = jnp.concatenate([z[pl.ds(at + NT, 32), tile], z[pl.ds(at + NT + 64, 32), tile]], axis=0)
            h = dot(both, vw[:, tile]) + own.astype(F32) * col_sum
            weighted = []
            for c in range(3):
                weighted.append((grad_i[c, low, tile] * h[0:32]).astype(BF16))
                weighted.append((grad_i[c, high, tile] * h[32:64]).astype(BF16))
            total = total + dot(jnp.concatenate(weighted, axis=0), inc_t[tile, :])
        return packed_planes(total)

    z_lo, y = t // 4, lax.rem(t, 4)
    is_owner = jnp.logical_or(z_lo == 1, z_lo == 2)
    mine = lax.rem(t + N_OWN - OWN0, N_OWN)
    far = jnp.where(z_lo <= 1, 2, 1)
    near = 3 - far
    to_owners = [(far, 2), (far, 1), (far, 3), (far, 0), (near, 2), (near, 1), (near, 3), (near, 0)]
    end = jnp.where(z_lo == 1, 3, 0)
    inner, edge = 3 - z_lo, 3 - end
    to_all = [
        (end, 2), (end, 1), (end, 3), (inner, 2), (edge, 2), (end, 0), (inner, 1), (inner, 3),
        (edge, 1), (edge, 3), (z_lo, 2), (inner, 0), (edge, 0), (z_lo, 1), (z_lo, 3),
    ]
    waits = []

    def spot_of(step):
        return step[0] * 4 + lax.rem(y + step[1], 4)

    def drain():
        while waits:
            waits.pop(0)()

    def adjoint_over_train(n, vector, extra=None, before=lambda: None, meanwhile=False):
        part, arrived, everything = s_part[n], s_in[n], s_all[n]
        adjoint(vector)

        def fill(plane):
            planes = adjoint_half(plane)
            for k in range(4):
                for c in range(3):
                    part[plane * 4 + k, c] = planes[c][k * 8 : (k + 1) * 8]
                if extra is not None:
                    part[plane * 4 + k, 3] = extra

        def scatter(d):
            owner = spot_of(to_owners[d])
            return pltpu.make_async_remote_copy(
                src_ref=part.at[owner - OWN0], dst_ref=arrived.at[t],
                send_sem=rs_send.at[n, d], recv_sem=rs_recv.at[n, t],
                device_id=(owner, i), device_id_type=MESH,
            )

        def gather(d):
            return pltpu.make_async_remote_copy(
                src_ref=everything.at[mine], dst_ref=everything.at[mine],
                send_sem=ag_send.at[n, d], recv_sem=ag_recv.at[n, mine],
                device_id=(spot_of(to_all[d]), i), device_id_type=MESH,
            )

        fill(far - 1)
        before()
        for d in range(4):
            scatter(d).start()
        fill(near - 1)
        for d in range(4, N_OWN - 1):
            scatter(d).start()

        @pl.when(jnp.logical_not(is_owner))
        def _():
            scatter(N_OWN - 1).start()

        drain()
        if meanwhile:
            vu[NI:, :] = z[NT:, :]
            diag, outer = matern(
                dot_nt(z[0:NT, :], z[NT:, :]), on_diagonal(gram_t[0:NT], 1), on_diagonal(gram_i, 0)
            )
            diag_ref[...] = diag.astype(BF16)
            outer_ref[...] = outer

        @pl.when(is_owner)
        def _():
            total = part[mine]
            for step in reversed(to_all):
                source = spot_of(step)
                pltpu.make_async_remote_copy(
                    src_ref=part.at[mine], dst_ref=arrived.at[source],
                    send_sem=rs_send.at[n, 0], recv_sem=rs_recv.at[n, source],
                    device_id=(source, i), device_id_type=MESH,
                ).wait_recv()
                total = total + arrived[source]
            everything[mine] = total
            for d in range(N_TRAIN - 1):
                gather(d).start()

        def arrive():
            for k in range(N_OWN):
                @pl.when(t != k + OWN0)
                def _():
                    pltpu.make_async_remote_copy(
                        src_ref=everything.at[k], dst_ref=everything.at[k],
                        send_sem=ag_send.at[n, 0], recv_sem=ag_recv.at[n, k],
                        device_id=(k + OWN0, i), device_id_type=MESH,
                    ).wait_recv()
            return [everything[:, c].reshape(64, 128) for c in range(3)]

        def finish():
            for d in range(N_OWN - 1):
                scatter(d).wait_send()

            @pl.when(jnp.logical_not(is_owner))
            def _():
                scatter(N_OWN - 1).wait_send()

            @pl.when(is_owner)
            def _():
                for d in range(N_TRAIN - 1):
                    gather(d).wait_send()

        waits.append(finish)
        return arrive

    has_chunk = x < P_OWN // 2
    in_plane_steps = [(2, 0), (2, 1), (1, 0), (3, 0), (1, 1), (3, 1), (0, 1)]

    def plane_spot(step):
        return lax.rem(x + step[0], 4) * 2 + lax.rem(core + step[1], 2)

    def sum_over_induce(n, planes):
        part, arrived, column, everything = p_part[n], p_in[n], p_z[n], p_all[n]
        for c in range(3):
            for r in range(4):
                part[c * 4 + r] = planes[c][r * 8 : (r + 1) * 8]

        def pair_of(k):
            return pl.ds(k * 2, 2)

        def scatter(d):
            k = plane_spot(in_plane_steps[d])
            return pltpu.make_async_remote_copy(
                src_ref=part.at[pair_of(k)], dst_ref=arrived.at[spot],
                send_sem=pr_send.at[n, d], recv_sem=pr_recv.at[n, spot],
                device_id=in_plane(k), device_id_type=MESH,
            )

        def across(d):
            return pltpu.make_async_remote_copy(
                src_ref=column.at[zh], dst_ref=column.at[zh],
                send_sem=pz_send.at[n, d], recv_sem=pz_recv.at[n, zh],
                device_id=in_column(lax.rem(zh + d, N_ZHI)), device_id_type=MESH,
            )

        def gather(d):
            return pltpu.make_async_remote_copy(
                src_ref=everything.at[pair_of(spot)], dst_ref=everything.at[pair_of(spot)],
                send_sem=pg_send.at[n, d], recv_sem=pg_recv.at[n, spot],
                device_id=in_plane(plane_spot(in_plane_steps[d])), device_id_type=MESH,
            )

        def for_owners(act):
            for d, step in enumerate(in_plane_steps):
                @pl.when(plane_spot(step) < P_OWN)
                def _():
                    act(d)

        for_owners(lambda d: scatter(d).start())
        drain()

        @pl.when(has_chunk)
        def _():
            total = part[pair_of(spot)]
            for step in reversed(in_plane_steps):
                source = plane_spot(step)
                pltpu.make_async_remote_copy(
                    src_ref=part.at[pair_of(spot)], dst_ref=arrived.at[source],
                    send_sem=pr_send.at[n, 0], recv_sem=pr_recv.at[n, source],
                    device_id=in_plane(source), device_id_type=MESH,
                ).wait_recv()
                total = total + arrived[source]
            column[zh] = total
            for d in (2, 1, 3):
                across(d).start()
            for d in (1, 3, 2):
                source = lax.rem(zh + d, N_ZHI)
                pltpu.make_async_remote_copy(
                    src_ref=column.at[zh], dst_ref=column.at[source],
                    send_sem=pz_send.at[n, 0], recv_sem=pz_recv.at[n, source],
                    device_id=in_column(source), device_id_type=MESH,
                ).wait_recv()
            everything[pair_of(spot)] = (column[0] + column[1]) + (column[2] + column[3])
            for d in range(N_PLANE - 1):
                gather(d).start()

        def arrived_from(d):
            k = plane_spot(in_plane_steps[d])
            pltpu.make_async_remote_copy(
                src_ref=everything.at[pair_of(k)], dst_ref=everything.at[pair_of(k)],
                send_sem=pg_send.at[n, 0], recv_sem=pg_recv.at[n, k],
                device_id=in_plane(k), device_id_type=MESH,
            ).wait_recv()

        def arrive():
            for_owners(arrived_from)
            return [everything[c * 4 : (c + 1) * 4].reshape(32, 128) for c in range(3)]

        def finish():
            for_owners(lambda d: scatter(d).wait_send())

            @pl.when(has_chunk)
            def _():
                for d in range(1, N_ZHI):
                    across(d).wait_send()
                for d in range(N_PLANE - 1):
                    gather(d).wait_send()

        waits.append(finish)
        return arrive

    def whole_sum(planes, others):
        line = sum(jnp.sum(a * b, axis=0, keepdims=True) for a, b in zip(planes, others))
        return jnp.sum(line, axis=1, keepdims=True)

    forces = pack(tf[...])

    def everyone_is_in():
        pl.semaphore_wait(barrier, N_TRAIN - 1 + N_PLANE - 1 + N_ZHI - 1)

    start = adjoint_over_train(0, forces, before=everyone_is_in, meanwhile=True)()
    probed = sum_over_induce(0, forward(start))()
    row8 = lax.broadcasted_iota(jnp.int32, (8, 128), 0)
    sums = jnp.where(row8 == 0, whole_sum(probed, probed), whole_sum(forces, probed))
    again = adjoint_over_train(1, probed, sums)()
    quotient = s_all1[0, 3, 0:1, 0:1] / s_all1[0, 3, 1:2, 0:1]
    center = 0.775 * quotient
    spread_ = 0.725 * quotient
    momentum = spread_ / center
    following = 1.0 / (2.0 * center / spread_ - momentum)
    direction = [a / center for a in start]
    residual = [a - b / center for a, b in zip(start, again)]
    turned = [following * momentum * a + 2.0 * following / spread_ * b for a, b in zip(direction, residual)]
    coeffs = [a + b for a, b in zip(direction, turned)]
    arrive = sum_over_induce(1, forward(turned))
    unpack_into(out_coeff, coeffs)
    rows = spread(coeffs)
    for j, tile in enumerate(TILES):
        width = min(TILE, DESC - j * TILE)
        out_desc[pl.ds(j * TILE, width), :] = to_desc(rows, grad_i, tile).T[0:width]
    stores = [
        pltpu.make_async_copy(source, target, store_sem.at[k])
        for k, (source, target) in enumerate(((out_desc, far_desc), (out_coeff, far_coeff), (out_resid, far_resid)))
    ]
    stores[0].start()
    stores[1].start()
    final = adjoint_over_train(2, arrive())()
    unpack_into(out_resid, [a - b for a, b in zip(residual, final)])
    stores[2].start()
    drain()
    for store in stores:
        store.wait()


def write_out(coeffs, resid, desc, out_coeffs, out_resid, out_desc, via_coeffs, via_resid, via_desc, in_sem, out_sem):
    parts = [(desc, via_desc, out_desc, k * DESC_PART, DESC_PART) for k in range(DESC // DESC_PART)]
    parts += [(coeffs, via_coeffs, out_coeffs, 0, 192), (resid, via_resid, out_resid, 0, 192)]
    ins, outs = [], []
    for k, (source, via, target, at, size) in enumerate(parts):
        rows = pl.ds(at, size)
        ins.append(pltpu.make_async_copy(source.at[rows], via.at[rows], in_sem.at[k]))
        outs.append(pltpu.make_async_copy(via.at[rows], target.at[rows], out_sem.at[k]))
    for copy in ins:
        copy.start()
    for first, second in zip(ins, outs):
        first.wait()
        second.start()
    for copy in outs:
        copy.wait()


def per_device(train_coords, induce_coords, train_forces, atom_pairs, length_scale):
    vmem, dma = pltpu.VMEM, pltpu.SemaphoreType.DMA
    whole = pl.BlockSpec(memory_space=pltpu.VMEM)
    scratch = [vmem((192, NI), F32), vmem((192, NI), F32), vmem((DESC, NI), F32)]
    scratch += [
        vmem((NT, 192), F32), vmem((192, NI), F32), vmem((NT, 192), F32), vmem((2, DESC), jnp.int32),
        vmem((2, PAD), jnp.int32), vmem((256, PAD), BF16), vmem((PAD, 128), BF16),
        vmem((3, NT, PAD), F32), vmem((3, NI, PAD), F32),
        vmem((NT + NI, PAD), BF16), vmem((2 * NI, PAD), BF16), vmem((2 * NT, PAD), BF16),
        vmem((NT, NI), BF16), vmem((NT, NI), F32),
        vmem((NI, NI), BF16), vmem((NI, 128), F32),
    ]
    deep = (3, 4, 3)
    scratch += [vmem((N_OWN, d, 8, 128), F32) for d in deep]
    scratch += [vmem((N_TRAIN, d, 8, 128), F32) for d in deep]
    scratch += [vmem((N_OWN, d, 8, 128), F32) for d in deep]
    scratch += [vmem((12, 8, 128), F32)] * 2
    scratch += [vmem((N_PLANE, 2, 8, 128), F32)] * 2
    scratch += [vmem((N_ZHI, 2, 8, 128), F32)] * 2
    scratch += [vmem((12, 8, 128), F32)] * 2
    scratch += [dma((3, N_OWN)), dma((3, N_TRAIN)), dma((3, N_TRAIN)), dma((3, N_OWN))]
    scratch += [dma((2, N_PLANE)), dma((2, N_PLANE)), dma((2, N_ZHI)), dma((2, N_ZHI)), dma((2, N_PLANE)), dma((2, N_PLANE)), dma((4,)), dma((3,))]
    results = pl.pallas_call(
        kernel,
        out_shape=(
            jax.ShapeDtypeStruct((192, NI), F32),
            jax.ShapeDtypeStruct((192, NI), F32),
            jax.ShapeDtypeStruct((DESC, NI), F32),
        ),
        in_specs=[pl.BlockSpec(memory_space=pltpu.HBM)] * 4 + [pl.BlockSpec(memory_space=pltpu.SMEM)],
        out_specs=(pl.BlockSpec(memory_space=pltpu.HBM),) * 3,
        scratch_shapes=scratch,
        compiler_params=pltpu.CompilerParams(
            collective_id=0, has_side_effects=True, vmem_limit_bytes=63 * 1024 * 1024
        ),
        cost_estimate=pl.CostEstimate(flops=2_000_000_000, bytes_accessed=2_000_000, transcendentals=1_000_000),
    )(train_coords, induce_coords.T, train_forces, atom_pairs, length_scale)
    coeffs, resid, desc = pl.pallas_call(
        write_out,
        out_shape=[jax.ShapeDtypeStruct(r.shape, r.dtype) for r in results],
        in_specs=[pl.BlockSpec(memory_space=pltpu.HBM)] * 3,
        out_specs=[pl.BlockSpec(memory_space=pltpu.HBM)] * 3,
        scratch_shapes=[vmem(r.shape, r.dtype) for r in results] + [dma((DESC // DESC_PART + 2,))] * 2,
    )(*results)
    return coeffs.T, resid.T, desc.T


def solution(mesh):
    in_specs = (P("train", None), P("induce", None), P("train", None), P(), P())
    out_specs = (P("induce", None), P("induce", None), P("induce", None))
    return jax.shard_map(
        per_device, mesh=mesh, in_specs=in_specs, out_specs=out_specs, check_vma=False
    )
```
